1024 devices in a mesh: dp: 4 (over y_hi), fsdp: 256 (over x, y_lo, z, core).
Axes of the slice: x: 8, y: 8 (y_hi: 4, y_lo: 2; y = y_hi * 2 + y_lo), z: 8, core: 2. Of those that a mesh axis runs over, the one named last changes fastest.
Arguments:
- actor_gate: bfloat16 [27648, 1024], P('fsdp', 'dp'), may hold values from -6 to 6
- actor_up: bfloat16 [27648, 1024], P('fsdp', 'dp'), may hold values from -6 to 6
- actor_cotangent: bfloat16 [1024, 5120], P(('dp', 'fsdp')), may hold values from -3 to 3
- actor_down: bfloat16 [27648, 5120], P('fsdp'), may hold values from -0.078125 to 0.078125
- critic_gate: bfloat16 [27648, 1024], P('fsdp', 'dp'), may hold values from -6 to 6
- critic_up: bfloat16 [27648, 1024], P('fsdp', 'dp'), may hold values from -6 to 6
- critic_cotangent: bfloat16 [1024, 5120], P(('dp', 'fsdp')), may hold values from -3 to 3
- critic_down: bfloat16 [27648, 5120], P('fsdp'), may hold values from -0.078125 to 0.078125
Outputs:
- actor_down_grad: float32 [27648, 5120], P('fsdp', 'dp')
- actor_gate_grad: bfloat16 [27648, 1024], P('fsdp', 'dp')
- actor_up_grad: bfloat16 [27648, 1024], P('fsdp', 'dp')
- critic_down_grad: float32 [27648, 5120], P('fsdp', 'dp')
- critic_gate_grad: bfloat16 [27648, 1024], P('fsdp', 'dp')
- critic_up_grad: bfloat16 [27648, 1024], P('fsdp', 'dp')
The draws below stay inside these ranges and needn't reach their ends.
All inputs are finite; a program needn't handle non-finite values.
Results may differ from the reference program's by a relative error of at most 0.012.
Values may be sent and summed in bfloat16 or wider, within the bound.
A program may use at most 64 MiB of HBM per device.

```python
import jax
import jax.numpy as jnp
from jax import lax

D = 5120
FF = 27648
GROUP_TOK = 256
TOKENS = 1024
N_DP = 4


def block_levels(stream_key, extent, pieces, low, top_value):
    gain, own = 1.0, jax.random.fold_in(stream_key, 6)
    for axis_at, blocks in pieces:
        heights = jnp.exp(jax.random.uniform(jax.random.fold_in(own, axis_at), (blocks,), jnp.float32, low / len(pieces), top_value / len(pieces)))
        gain = gain * jnp.repeat(heights, extent[axis_at] // blocks).reshape([-1 if axis == axis_at else 1 for axis in range(len(extent))])
    return gain


def gaussian(stream_key, shape, deviation, limit, split=(), dtype=jnp.bfloat16):
    gain = block_levels(stream_key, shape, split, -0.22, 0.18) if split else 1.0
    result = jax.random.normal(stream_key, shape, jnp.float32) * deviation * gain
    return jnp.minimum(jnp.maximum(result, -limit), limit).astype(dtype)


def setup_inputs(seed: int = 0) -> dict:
    key_list = jax.random.split(jax.random.key(seed), 9)
    actor_gate = gaussian(key_list[0], (FF, TOKENS), 1.5, 6.0, ((0, 256), (1, 4)))
    actor_up = gaussian(key_list[1], (FF, TOKENS), 1.0, 6.0, ((0, 256), (1, 4)))
    actor_cotangent = gaussian(key_list[2], (TOKENS, D), 0.2, 3.0, ((0, 1024),))
    actor_down = gaussian(key_list[3], (FF, D), D ** -0.5, 0.078125, ((0, 256),))
    critic_gate = gaussian(key_list[4], (FF, TOKENS), 1.5, 6.0, ((0, 256), (1, 4)))
    critic_up = gaussian(key_list[5], (FF, TOKENS), 1.0, 6.0, ((0, 256), (1, 4)))
    critic_cotangent = gaussian(key_list[6], (TOKENS, D), 0.2, 3.0, ((0, 1024),))
    critic_down = gaussian(key_list[7], (FF, D), D ** -0.5, 0.078125, ((0, 256),))
    return dict(actor_gate=actor_gate, actor_up=actor_up, actor_cotangent=actor_cotangent, actor_down=actor_down, critic_gate=critic_gate, critic_up=critic_up, critic_cotangent=critic_cotangent, critic_down=critic_down)


def model_grads(gate, up, cotangent, down):
    gate32 = gate.astype(jnp.float32)
    up32 = up.astype(jnp.float32)
    sig = jax.nn.sigmoid(gate32)
    silu_val = gate32 * sig
    hidden = (silu_val * up32).astype(jnp.bfloat16)
    weight_grad = jnp.zeros(down.shape, jnp.float32)
    for group in range(N_DP):
        h_block = hidden[:, group * GROUP_TOK:(group + 1) * GROUP_TOK]
        c_block = cotangent[group * GROUP_TOK:(group + 1) * GROUP_TOK, :]
        partial_sum = jnp.dot(h_block, c_block, preferred_element_type=jnp.float32).astype(jnp.bfloat16)
        weight_grad = weight_grad + partial_sum.astype(jnp.float32)
    hidden_grad = lax.dot_general(down, cotangent, (((1,), (1,)), ((), ())), preferred_element_type=jnp.float32)
    gate_grad = (hidden_grad * up32 * sig * (1.0 + gate32 * (1.0 - sig))).astype(jnp.bfloat16)
    up_grad = (hidden_grad * silu_val).astype(jnp.bfloat16)
    return weight_grad, gate_grad, up_grad


def reference(actor_gate, actor_up, actor_cotangent, actor_down, critic_gate, critic_up, critic_cotangent, critic_down):
    actor_w, actor_g, actor_u = model_grads(actor_gate, actor_up, actor_cotangent, actor_down)
    critic_w, critic_g, critic_u = model_grads(critic_gate, critic_up, critic_cotangent, critic_down)
    return (actor_w, actor_g, actor_u, critic_w, critic_g, critic_u)
```

```python
import jax
import jax.numpy as jnp
from jax import lax
from jax.experimental import pallas as pl
from jax.experimental.pallas import tpu as pltpu
from jax.sharding import PartitionSpec as P

MESH = pl.DeviceIdType.MESH
BF16, F32 = jnp.bfloat16, jnp.float32

N_DP, NX, NLO, NZ = 4, 8, 2, 8
FF, TOK, D = 108, 256, 5120
COLS = D // N_DP
HALF = COLS // 2
PAD = 112
ROWS = 2 * PAD


def fsdp_index(x, lo, z, core):
    return ((x * NLO + lo) * NZ + z) * 2 + core


def permutation():
    j = lax.broadcasted_iota(jnp.int32, (TOK, TOK), 0)
    place = lax.broadcasted_iota(jnp.int32, (TOK, TOK), 1)
    moved = ((j >> 3) & 1) * 128 + (j >> 5) * 16 + ((j >> 4) & 1) * 8 + (j & 7)
    return jnp.where(moved == place, 1.0, 0.0).astype(BF16)


def kernel(
    a_gate, a_up, a_cot, a_down, c_gate, c_up, c_cot, c_down,
    a_w, a_g, a_u, c_w, c_g, c_u,
    row_in, row_out, row_got, stage,
    gate2, up2, down2, down, gate_p, up_p, hid, cot_a, cot_b,
    hacc, wacc_a, wacc_b, wout, hsend, hgot, gout, uout,
    load_sem, sib_send, sib_recv, p0_send, p0_recv, p1_send, p1_recv,
    ring_send, ring_recv, hid_send, hid_recv, rs_send, rs_recv, out_sem, out_send, out_recv,
):
    k = lax.axis_index("dp")
    f = lax.axis_index("fsdp")
    core = f % 2
    z = (f // 2) % NZ
    lo = (f // (2 * NZ)) % NLO
    x = f // (2 * NZ * NLO)
    zq, zs = z // 4, z % 4
    sib = (k, f + 1 - 2 * core)

    def by_core(fn):
        @pl.when(core == 0)
        def _():
            fn(0)

        @pl.when(core == 1)
        def _():
            fn(1)

    gates, ups, downs = (a_gate, c_gate), (a_up, c_up), (a_down, c_down)
    cot_rows = (a_cot, c_cot)
    columns = pl.ds(pl.multiple_of(k * COLS, 128), COLS)

    row_loads = [pltpu.make_async_copy(cot_rows[m], row_in.at[m], load_sem.at[m]) for m in range(2)]
    for copy in row_loads:
        copy.start()

    def own_loads(m):
        return (
            pltpu.make_async_copy(gates[m], gate2.at[m], load_sem.at[2]),
            pltpu.make_async_copy(ups[m], up2.at[m], load_sem.at[3]),
            pltpu.make_async_copy(downs[m].at[:, columns], down2.at[m], load_sem.at[4]),
        )

    by_core(lambda m: [copy.start() for copy in own_loads(m)])

    barrier = pltpu.get_barrier_semaphore()

    def greet(dp, fs):
        pl.semaphore_signal(barrier, inc=1, device_id=(dp, fs), device_id_type=MESH)

    own_p0 = zs == k
    for s in range(16):
        s_lo, s_z, s_core = s // 8, (s // 2) % 4, s % 2
        source = fsdp_index(x, s_lo, zq * 4 + s_z, s_core)

        @pl.when(jnp.logical_not((zs == k) & (source == f)))
        def _():
            greet(zs, source)

    for d in range(1, 8):
        greet(k, fsdp_index((x + d) % NX, lo, z, core))
        greet(k, fsdp_index(x, lo, (z + d) % NZ, core))
    for d in range(1, 4):
        greet((k + d) % N_DP, f)
    greet(*sib)

    for m in range(2):
        row_loads[m].wait()
        for b in range(N_DP):
            row_out[2 * b + m] = row_in[m, :, b * COLS:(b + 1) * COLS].astype(F32)

    pl.semaphore_wait(barrier, 34 - jnp.where(own_p0, 1, 0))

    mine = lo * 8 + zs * 2 + core
    stage0 = []
    for t in range(16):
        t_k, t_lo, t_core = t // 4, (t // 2) % 2, t % 2
        target = fsdp_index(x, t_lo, zq * 4 + k, t_core)
        is_self = (k == t_k) & (target == f)
        remote = pltpu.make_async_remote_copy(
            row_out.at[2 * t_k + t_core], row_got.at[mine], p0_send.at[t], p0_recv,
            device_id=(t_k, target), device_id_type=MESH)
        stage0.append((is_self, remote))

        @pl.when(is_self)
        def _(t_k=t_k, t_core=t_core):
            pltpu.make_async_copy(row_out.at[2 * t_k + t_core], row_got.at[mine], p0_recv).start()

        @pl.when(jnp.logical_not(is_self))
        def _(remote=remote):
            remote.start()

    def sibling_pushes(m):
        other = 1 - m
        return [
            pltpu.make_async_remote_copy(src, dst.at[m], sib_send.at[i], sib_recv.at[i], device_id=sib, device_id_type=MESH)
            for i, (src, dst) in enumerate((
                (gates[other], gate2), (ups[other], up2), (downs[other].at[:, columns], down2)))
        ]

    by_core(lambda m: [copy.start() for copy in sibling_pushes(m)])

    perm = permutation()

    pltpu.make_async_copy(row_got, row_got, p0_recv).wait()
    for r in range(16):
        stage[r:r + 1, :] = row_got[r]
    block = stage[...].astype(BF16)
    cot_a[z, x] = block[:, :HALF]
    cot_b[z, x] = block[:, HALF:]

    stage1 = []
    for d in range(1, 8):
        for i, (buf, target) in enumerate((
                (cot_a, fsdp_index((x + d) % NX, lo, z, core)), (cot_b, fsdp_index(x, lo, (z + d) % NZ, core)))):
            copy = pltpu.make_async_remote_copy(
                buf.at[z, x], buf.at[z, x], p1_send.at[i, d - 1], p1_recv.at[i], device_id=(k, target), device_id_type=MESH)
            copy.start()
            stage1.append(copy)

    def own_waits(m):
        for copy in own_loads(m):
            copy.wait()

    by_core(own_waits)
    by_core(lambda m: [copy.wait() for copy in sibling_pushes(m)])
    for h in range(2):
        rows = slice(h * PAD, h * PAD + FF)
        gate32 = jnp.dot(gate2[h], perm, preferred_element_type=F32)
        up32 = jnp.dot(up2[h], perm, preferred_element_type=F32)
        gate_p[rows, :] = gate32
        up_p[rows, :] = up32
        hidden = (gate32 * jax.nn.sigmoid(gate32) * up32).astype(BF16)
        hid[k, 0, rows, :] = hidden[:, :128]
        hid[k, 1, rows, :] = hidden[:, 128:]
        down[rows, :] = down2[h]

    hid_copies = []
    for d in range(1, 4):
        copy = pltpu.make_async_remote_copy(
            hid.at[k], hid.at[k], hid_send.at[d - 1], hid_recv.at[d - 1],
            device_id=((k + d) % N_DP, f), device_id_type=MESH)
        copy.start()
        hid_copies.append(copy)

    for i, buf in enumerate((cot_a, cot_b)):
        whole = buf.at[0, pl.ds(0, 7)]
        pltpu.make_async_copy(whole, whole, p1_recv.at[i]).wait()

    def ring_copy(flow, step):
        forward = flow % 2 == 0
        shift = -step if forward else step
        if flow < 2:
            unit = (z + shift + NZ) % NZ
            ref = cot_a.at[unit] if step < 3 else cot_a.at[unit, pl.ds(0 if forward else 4, 4)]
            target = fsdp_index(x, lo, (z + (1 if forward else NZ - 1)) % NZ, core)
        else:
            unit = (x + shift + NX) % NX
            ref = cot_b.at[:, unit] if step < 3 else cot_b.at[pl.ds(0 if forward else 4, 4), unit]
            target = fsdp_index((x + (1 if forward else NX - 1)) % NX, lo, z, core)
        return pltpu.make_async_remote_copy(
            ref, ref, ring_send.at[flow, step], ring_recv.at[flow, step], device_id=(k, target), device_id_type=MESH)

    rings = []
    for step in range(4):
        for flow in range(4):
            if step:
                rings[4 * (step - 1) + flow].wait_recv()
            copy = ring_copy(flow, step)
            copy.start()
            rings.append(copy)
    for flow in range(4):
        rings[12 + flow].wait_recv()

    def hidden_partial(unit):
        both = []
        for buf, part in ((cot_a, slice(0, HALF)), (cot_b, slice(HALF, COLS))):
            both.append(lax.dot_general(
                down[:, part], buf[unit].reshape(128, HALF), (((1,), (1,)), ((), ())), preferred_element_type=F32))
        return both[0] + both[1]

    rs_copies = []
    for d in range(1, 4):
        group = (k + d) % N_DP
        for q in range(2):
            hsend[d - 1, q] = hidden_partial(q * 4 + group).astype(BF16)
        copy = pltpu.make_async_remote_copy(
            hsend.at[d - 1], hgot.at[d - 1], rs_send.at[d - 1], rs_recv.at[d - 1], device_id=(group, f), device_id_type=MESH)
        copy.start()
        rs_copies.append(copy)
    for q in range(2):
        hacc[q] = hidden_partial(q * 4 + k)

    for copy in hid_copies:
        copy.wait_recv()
    for buf, acc, part in ((cot_a, wacc_a, slice(0, HALF)), (cot_b, wacc_b, slice(HALF, COLS))):
        for unit in range(8):
            term = jnp.dot(hid[unit % 4, unit // 4], buf[unit].reshape(128, HALF), preferred_element_type=F32)
            if unit == 0:
                acc[...] = term
            elif unit < 7:
                acc[...] += term
            else:
                term = acc[...] + term
                wout[0, :, part] = term[:FF]
                wout[1, :, part] = term[PAD:PAD + FF]

    weights, ggrads, ugrads = (a_w, c_w), (a_g, c_g), (a_u, c_u)

    def out_copies(m, i, src, outs):
        return (
            pltpu.make_async_copy(src.at[m], outs[m], out_sem.at[i]),
            pltpu.make_async_remote_copy(
                src.at[1 - m], outs[m], out_send.at[i], out_recv.at[i], device_id=sib, device_id_type=MESH),
        )

    by_core(lambda m: [copy.start() for copy in out_copies(m, 0, wout, weights)])

    for copy in rs_copies:
        copy.wait_recv()
    halves_g, halves_u = [], []
    for q in range(2):
        lanes = slice(q * 128, (q + 1) * 128)
        grad = hacc[q] + hgot[0, q].astype(F32) + hgot[1, q].astype(F32) + hgot[2, q].astype(F32)
        gate32, up32 = gate_p[:, lanes], up_p[:, lanes]
        sig = jax.nn.sigmoid(gate32)
        halves_g.append((grad * up32 * sig * (1.0 + gate32 * (1.0 - sig))).astype(BF16))
        halves_u.append((grad * (gate32 * sig)).astype(BF16))
    perm = permutation()
    for halves, out in ((halves_g, gout), (halves_u, uout)):
        back = lax.dot_general(
            jnp.concatenate(halves, axis=1), perm, (((1,), (1,)), ((), ())), preferred_element_type=F32).astype(BF16)
        out[0] = back[:FF]
        out[1] = back[PAD:PAD + FF]

    by_core(lambda m: [copy.start() for copy in out_copies(m, 1, gout, ggrads)])
    by_core(lambda m: [copy.start() for copy in out_copies(m, 2, uout, ugrads)])

    for is_self, copy in stage0:
        @pl.when(jnp.logical_not(is_self))
        def _(copy=copy):
            copy.wait_send()
    for copy in stage1 + hid_copies + rings + rs_copies:
        copy.wait_send()

    def finish(m):
        for i, (src, outs) in enumerate(((wout, weights), (gout, ggrads), (uout, ugrads))):
            local, remote = out_copies(m, i, src, outs)
            local.wait()
            remote.wait_send()
            pltpu.make_async_remote_copy(
                src.at[m], outs[1 - m], out_send.at[i], out_recv.at[i], device_id=sib, device_id_type=MESH).wait_recv()

    by_core(finish)


def on_device(*args):
    any_spec = pl.BlockSpec(memory_space=pl.ANY)
    dma, vmem = pltpu.SemaphoreType.DMA, pltpu.VMEM
    weight = jax.ShapeDtypeStruct((FF, COLS), F32)
    small = jax.ShapeDtypeStruct((FF, TOK), BF16)
    return pl.pallas_call(
        kernel,
        out_shape=(weight, small, small, weight, small, small),
        in_specs=[any_spec] * 8,
        out_specs=(any_spec,) * 6,
        scratch_shapes=[
            vmem((2, 1, D), BF16),
            vmem((8, 1, COLS), F32),
            vmem((16, 1, COLS), F32),
            vmem((16, COLS), F32),
            vmem((2, FF, TOK), BF16),
            vmem((2, FF, TOK), BF16),
            vmem((2, FF, COLS), BF16),
            vmem((ROWS, COLS), BF16),
            vmem((ROWS, TOK), F32),
            vmem((ROWS, TOK), F32),
            vmem((N_DP, 2, ROWS, 128), BF16),
            vmem((NZ, NX, 16, HALF), BF16),
            vmem((NZ, NX, 16, HALF), BF16),
            vmem((2, ROWS, 128), F32),
            vmem((ROWS, HALF), F32),
            vmem((ROWS, HALF), F32),
            vmem((2, FF, COLS), F32),
            vmem((3, 2, ROWS, 128), BF16),
            vmem((3, 2, ROWS, 128), BF16),
            vmem((2, FF, TOK), BF16),
            vmem((2, FF, TOK), BF16),
            dma((5,)),
            dma((3,)),
            dma((3,)),
            dma((16,)),
            dma,
            dma((2, 7)),
            dma((2,)),
            dma((4, 4)),
            dma((4, 4)),
            dma((3,)),
            dma((3,)),
            dma((3,)),
            dma((3,)),
            dma((3,)),
            dma((3,)),
            dma((3,)),
        ],
        compiler_params=pltpu.CompilerParams(
            collective_id=0, has_side_effects=True, vmem_limit_bytes=40 * 1024 * 1024),
        cost_estimate=pl.CostEstimate(flops=1_200_000_000, bytes_accessed=4_000_000, transcendentals=200_000),
        name="mlp_backward",
    )(*args)


def solution(mesh):
    placed = (
        P("fsdp", "dp"),
        P("fsdp", "dp"),
        P(("dp", "fsdp"), None),
        P("fsdp", None),
    )
    return jax.shard_map(
        on_device,
        mesh=mesh,
        in_specs=placed * 2,
        out_specs=(P("fsdp", "dp"),) * 6,
        check_vma=False,
    )
```

```python
import jax
import jax.numpy as jnp
from jax import lax
from jax.experimental import pallas as pl
from jax.experimental.pallas import tpu as pltpu
from jax.sharding import PartitionSpec as P

MESH = pl.DeviceIdType.MESH
BF16, F32 = jnp.bfloat16, jnp.float32

N_DP, NX, NLO, NZ = 4, 8, 2, 8
FF, TOK, D = 108, 256, 5120
COLS = D // N_DP
PAD = 112
ROWS = 2 * PAD
LANES = 256
CHUNKS = 2
PART = 4 // CHUNKS
VMEM_LIMIT = 58 * 1024 * 1024


def fsdp_index(x, lo, z, core):
    return ((x * NLO + lo) * NZ + z) * 2 + core


def permutation(k):
    j = lax.broadcasted_iota(jnp.int32, (TOK, TOK), 0)
    place = lax.broadcasted_iota(jnp.int32, (TOK, TOK), 1)
    kind = ((j >> 5) + k) & 1
    moved = ((j >> 3) & 1) * 128 + kind * 64 + (j >> 6) * 16 + ((j >> 4) & 1) * 8 + (j & 7)
    return jnp.where(moved == place, 1.0, 0.0).astype(BF16)


def kernel(
    a_gate, a_up, a_cot, a_down, c_gate, c_up, c_cot, c_down,
    a_w, a_g, a_u, c_w, c_g, c_u,
    row_in, row_out, row_got, stage,
    gate2, up2, down2, down, gate_f, up_f, hid, cot,
    hown, hsend_a, hsend_b, hgot, wout, gout, uout,
    load_sem, sib_send, sib_recv, p0_send, p0_recv, p1_send, p1_recv,
    ring_send, ring_recv, hid_send, hid_recv, rs_send, rs_recv, out_sem, out_send, out_recv,
):
    k = lax.axis_index("dp")
    f = lax.axis_index("fsdp")
    core = f % 2
    z = (f // 2) % NZ
    lo = (f // (2 * NZ)) % NLO
    x = f // (2 * NZ * NLO)
    zq, zs = z // 4, z % 4
    kind, xh = (x + z) % 2, x // 2
    sib = (k, f + 1 - 2 * core)

    def by_core(fn):
        @pl.when(core == 0)
        def _():
            fn(0)

        @pl.when(core == 1)
        def _():
            fn(1)

    gates, ups, downs = (a_gate, c_gate), (a_up, c_up), (a_down, c_down)
    cot_rows = (a_cot, c_cot)
    columns = pl.ds(pl.multiple_of(k * COLS, 128), COLS)

    row_loads = [pltpu.make_async_copy(cot_rows[m], row_in.at[m], load_sem.at[m]) for m in range(2)]
    for copy in row_loads:
        copy.start()

    def own_loads(m):
        return (
            pltpu.make_async_copy(gates[m], gate2.at[m], load_sem.at[2]),
            pltpu.make_async_copy(ups[m], up2.at[m], load_sem.at[3]),
            pltpu.make_async_copy(downs[m].at[:, columns], down2.at[m], load_sem.at[4]),
        )

    by_core(lambda m: [copy.start() for copy in own_loads(m)])

    barrier = pltpu.get_barrier_semaphore()

    def greet(dp, fs):
        pl.semaphore_signal(barrier, inc=1, device_id=(dp, fs), device_id_type=MESH)

    own_p0 = zs == k
    for s in range(16):
        s_lo, s_z, s_core = s // 8, (s // 2) % 4, s % 2
        source = fsdp_index(x, s_lo, zq * 4 + s_z, s_core)

        @pl.when(jnp.logical_not((zs == k) & (source == f)))
        def _():
            greet(zs, source)

    for i in range(4):
        @pl.when((kind == 1) | (i > 0))
        def _(i=i):
            greet(k, fsdp_index((x + 2 * i + kind) % NX, lo, z, core))

        @pl.when((kind == 0) | (i > 0))
        def _(i=i):
            greet(k, fsdp_index(x, lo, (z + 2 * i + 1 - kind) % NZ, core))

    for step in (1, NX - 1):
        greet(k, fsdp_index((x + step) % NX, lo, z, core))
        greet(k, fsdp_index(x, lo, (z + step) % NZ, core))
    for d in range(1, 4):
        greet((k + d) % N_DP, f)
    greet(*sib)

    for m in range(2):
        row_loads[m].wait()
        for b in range(N_DP):
            row_out[2 * b + m] = row_in[m, :, b * COLS:(b + 1) * COLS].astype(F32)

    pl.semaphore_wait(barrier, 31 - jnp.where(own_p0, 1, 0))

    mine = lo * 8 + zs * 2 + core
    stage0 = []
    for t in range(16):
        t_k, t_lo, t_core = t // 4, (t // 2) % 2, t % 2
        target = fsdp_index(x, t_lo, zq * 4 + k, t_core)
        is_self = (k == t_k) & (target == f)
        remote = pltpu.make_async_remote_copy(
            row_out.at[2 * t_k + t_core], row_got.at[mine], p0_send.at[t], p0_recv,
            device_id=(t_k, target), device_id_type=MESH)
        stage0.append((is_self, remote))

        @pl.when(is_self)
        def _(t_k=t_k, t_core=t_core):
            pltpu.make_async_copy(row_out.at[2 * t_k + t_core], row_got.at[mine], p0_recv).start()

        @pl.when(jnp.logical_not(is_self))
        def _(remote=remote):
            remote.start()

    def sibling_pushes(m):
        other = 1 - m
        return [
            pltpu.make_async_remote_copy(src, dst.at[m], sib_send.at[i], sib_recv.at[i], device_id=sib, device_id_type=MESH)
            for i, (src, dst) in enumerate((
                (gates[other], gate2), (ups[other], up2), (downs[other].at[:, columns], down2)))
        ]

    by_core(lambda m: [copy.start() for copy in sibling_pushes(m)])

    perm = permutation(k)

    pltpu.make_async_copy(row_got, row_got, p0_recv).wait()
    for r in range(16):
        stage[r:r + 1, :] = row_got[r]
    cot[zq, zs // 2, zs % 2, kind, xh] = stage[...].astype(BF16)

    own_block = cot.at[zq, zs // 2, zs % 2, kind, xh]
    stage1 = []
    for d in (4, 5, 3, 6, 2, 7, 1):
        target = jnp.where(
            kind == 0, fsdp_index((x + d) % NX, lo, z, core), fsdp_index(x, lo, (z + d) % NZ, core))
        copy = pltpu.make_async_remote_copy(
            own_block, own_block, p1_send.at[d - 1], p1_recv.at[kind], device_id=(k, target), device_id_type=MESH)
        copy.start()
        stage1.append(copy)

    def own_waits(m):
        for copy in own_loads(m):
            copy.wait()

    by_core(own_waits)
    by_core(lambda m: [copy.wait() for copy in sibling_pushes(m)])
    for h in range(2):
        rows = slice(h * PAD, h * PAD + FF)
        gate32 = jnp.dot(gate2[h], perm, preferred_element_type=F32)
        up32 = jnp.dot(up2[h], perm, preferred_element_type=F32)
        hidden = (gate32 * jax.nn.sigmoid(gate32) * up32).astype(BF16)
        hid[k, 0, rows, :] = hidden[:, :128]
        hid[k, 1, rows, :] = hidden[:, 128:]
        down[h * 128:h * 128 + FF, :] = down2[h]

    hid_copies = []
    for d in range(1, 4):
        copy = pltpu.make_async_remote_copy(
            hid.at[k], hid.at[k], hid_send.at[d - 1], hid_recv.at[d - 1],
            device_id=((k + d) % N_DP, f), device_id_type=MESH)
        copy.start()
        hid_copies.append(copy)

    for i in range(2):
        three, four = cot.at[0, 0, 0, 0, pl.ds(0, 3)], cot.at[0, 0, 0, 0]

        @pl.when(kind == i)
        def _(i=i, three=three):
            pltpu.make_async_copy(three, three, p1_recv.at[i]).wait()

        @pl.when(kind != i)
        def _(i=i, four=four):
            pltpu.make_async_copy(four, four, p1_recv.at[i]).wait()

    def ring_copy(flow, chunk, step):
        forward = flow % 2 == 0
        shift = -step if forward else step
        part = pl.ds(chunk * PART, PART)
        if flow < 2:
            unit = (z + shift + NZ) % NZ
            ref = cot.at[unit // 4, (unit // 2) % 2, unit % 2, 0, part]
            target = fsdp_index(x, lo, (z + (1 if forward else NZ - 1)) % NZ, core)
        else:
            unit = (x + shift + NX) % NX
            ref = cot.at[chunk, :, 1 - unit % 2, 1, unit // 2]
            target = fsdp_index((x + (1 if forward else NX - 1)) % NX, lo, z, core)
        return pltpu.make_async_remote_copy(
            ref, ref, ring_send.at[flow, chunk, step], ring_recv.at[flow, chunk, step],
            device_id=(k, target), device_id_type=MESH)

    def hidden_partial(block):
        return lax.dot_general(
            block.reshape(64, COLS), down[...], (((1,), (1,)), ((), ())), preferred_element_type=F32)

    def to_group(group, src, piece):
        apart = (group + N_DP - k) % N_DP

        @pl.when(apart != 0)
        def _():
            pltpu.make_async_remote_copy(
                src, piece(hgot.at[apart - 1]), rs_send, rs_recv, device_id=(group, f), device_id_type=MESH).start()

        return apart == 0

    def unit_a(unit):
        unit = (unit + NZ) % NZ
        group, q = unit % 4, unit // 4
        grad = hidden_partial(cot[q, group // 2, group % 2, 0]).reshape(4, 16, LANES)
        hsend_a[unit] = grad.astype(BF16)

        @pl.when(to_group(group, hsend_a.at[unit], lambda ref: ref.at[q, 0]))
        def _():
            hown[q, 0] = grad

    def unit_b(unit):
        unit = (unit + NX) % NX
        low = 1 - unit % 2
        grad = hidden_partial(cot[:, :, low, 1, unit // 2]).reshape(2, 2, 16, LANES)
        hsend_b[unit] = grad.astype(BF16)
        for high in range(2):
            @pl.when(to_group(2 * high + low, hsend_b.at[unit, :, high], lambda ref: ref.at[:, 1, unit // 2]))
            def _(high=high):
                hown[:, 1, unit // 2] = grad[:, high]

    rings = {}
    for step in range(5):
        for chunk in range(CHUNKS):
            for flow in range(4):
                if (flow, chunk, step - 1) in rings:
                    rings[flow, chunk, step - 1].wait_recv()
                if step < 3 or step == 3 and (chunk < CHUNKS // 2) == (flow % 2 == 0):
                    rings[flow, chunk, step] = ring_copy(flow, chunk, step)
                    rings[flow, chunk, step].start()
        if step == 0:
            for h in range(2):
                gate32 = lax.dot_general(perm, gate2[h], (((0,), (1,)), ((), ())), preferred_element_type=F32)
                up32 = lax.dot_general(perm, up2[h], (((0,), (1,)), ((), ())), preferred_element_type=F32)
                sig = jax.nn.sigmoid(gate32)
                gate_f[:, h * 128:h * 128 + FF] = up32 * sig * (1.0 + gate32 * (1.0 - sig))
                up_f[:, h * 128:h * 128 + FF] = gate32 * sig
        for shift in (-step, step) if 0 < step < 4 else (step,):
            unit_a(z + shift)
            unit_b(x + shift)

    for copy in hid_copies:
        copy.wait_recv()
    for n in range(COLS // 256):
        part = slice(n * 256, (n + 1) * 256)
        total = None
        for group in range(N_DP):
            left = jnp.concatenate([hid[group, 0], hid[group, 1]], axis=1)
            right = jnp.concatenate(
                [cot[q, group // 2, group % 2, :, :, :, part].reshape(128, 256) for q in range(2)], axis=0)
            term = jnp.dot(left, right, preferred_element_type=F32)
            total = term if total is None else total + term
        wout[0, :, part] = total[:FF]
        wout[1, :, part] = total[PAD:PAD + FF]

    weights, ggrads, ugrads = (a_w, c_w), (a_g, c_g), (a_u, c_u)

    def out_copies(m, i, src, outs):
        return (
            pltpu.make_async_copy(src.at[m], outs[m], out_sem.at[i]),
            pltpu.make_async_remote_copy(
                src.at[1 - m], outs[m], out_send.at[i], out_recv.at[i], device_id=sib, device_id_type=MESH),
        )

    by_core(lambda m: [copy.start() for copy in out_copies(m, 0, wout, weights)])

    pltpu.make_async_copy(hgot, hgot, rs_recv).wait()
    grad = hown[...]
    for i in range(3):
        grad = grad + hgot[i].astype(F32)
    grad = grad.reshape(TOK, LANES)
    perm = permutation(k)
    for factor, out in ((gate_f, gout), (up_f, uout)):
        back = lax.dot_general(
            (grad * factor[...]).astype(BF16), perm, (((0,), (1,)), ((), ())), preferred_element_type=F32).astype(BF16)
        out[0] = back[:FF]
        out[1] = back[128:128 + FF]

    by_core(lambda m: [copy.start() for copy in out_copies(m, 1, gout, ggrads)])
    by_core(lambda m: [copy.start() for copy in out_copies(m, 2, uout, ugrads)])

    for is_self, copy in stage0:
        @pl.when(jnp.logical_not(is_self))
        def _(copy=copy):
            copy.wait_send()
    for copy in stage1 + hid_copies + list(rings.values()):
        copy.wait_send()
    pltpu.make_async_copy(hgot, hgot, rs_send).wait()

    def finish(m):
        for i, (src, outs) in enumerate(((wout, weights), (gout, ggrads), (uout, ugrads))):
            local, remote = out_copies(m, i, src, outs)
            local.wait()
            remote.wait_send()
            pltpu.make_async_remote_copy(
                src.at[m], outs[1 - m], out_send.at[i], out_recv.at[i], device_id=sib, device_id_type=MESH).wait_recv()

    by_core(finish)


def store(*refs):
    ins, outs, held, (in_sem, out_sem) = refs[:6], refs[6:12], refs[12:18], refs[18:]
    loads = [pltpu.make_async_copy(ins[i], held[i], in_sem.at[i]) for i in range(6)]
    stores = [pltpu.make_async_copy(held[i], outs[i], out_sem.at[i]) for i in range(6)]
    for copy in loads:
        copy.start()
    for load, copy in zip(loads, stores):
        load.wait()
        copy.start()
    for copy in stores:
        copy.wait()


def on_device(*args):
    hbm_spec = pl.BlockSpec(memory_space=pltpu.HBM)
    dma, vmem = pltpu.SemaphoreType.DMA, pltpu.VMEM
    weight = jax.ShapeDtypeStruct((FF, COLS), F32)
    small = jax.ShapeDtypeStruct((FF, TOK), BF16)
    results = pl.pallas_call(
        kernel,
        out_shape=(weight, small, small, weight, small, small),
        in_specs=[hbm_spec] * 8,
        out_specs=(hbm_spec,) * 6,
        scratch_shapes=[
            vmem((2, 1, D), BF16),
            vmem((8, 1, COLS), F32),
            vmem((16, 1, COLS), F32),
            vmem((16, COLS), F32),
            vmem((2, FF, TOK), BF16),
            vmem((2, FF, TOK), BF16),
            vmem((2, FF, COLS), BF16),
            vmem((LANES, COLS), BF16),
            vmem((TOK, LANES), F32),
            vmem((TOK, LANES), F32),
            vmem((N_DP, 2, ROWS, 128), BF16),
            vmem((2, 2, 2, 2, 4, 16, COLS), BF16),
            vmem((2, 2, 4, 16, LANES), F32),
            vmem((NZ, 4, 16, LANES), BF16),
            vmem((NX, 2, 2, 16, LANES), BF16),
            vmem((3, 2, 2, 4, 16, LANES), BF16),
            vmem((2, FF, COLS), F32),
            vmem((2, FF, TOK), BF16),
            vmem((2, FF, TOK), BF16),
            dma((5,)),
            dma((3,)),
            dma((3,)),
            dma((16,)),
            dma,
            dma((7,)),
            dma((2,)),
            dma((4, CHUNKS, 4)),
            dma((4, CHUNKS, 4)),
            dma((3,)),
            dma((3,)),
            dma,
            dma,
            dma((3,)),
            dma((3,)),
            dma((3,)),
        ],
        compiler_params=pltpu.CompilerParams(
            collective_id=0, has_side_effects=True, vmem_limit_bytes=VMEM_LIMIT),
        cost_estimate=pl.CostEstimate(flops=1_200_000_000, bytes_accessed=4_000_000, transcendentals=200_000),
        name="mlp_backward",
    )(*args)
    return pl.pallas_call(
        store,
        out_shape=(weight, small, small, weight, small, small),
        in_specs=[hbm_spec] * 6,
        out_specs=(hbm_spec,) * 6,
        scratch_shapes=[vmem(a.shape, a.dtype) for a in results] + [dma((6,)), dma((6,))],
        compiler_params=pltpu.CompilerParams(vmem_limit_bytes=VMEM_LIMIT),
        name="store_results",
    )(*results)


def solution(mesh):
    placed = (
        P("fsdp", "dp"),
        P("fsdp", "dp"),
        P(("dp", "fsdp"), None),
        P("fsdp", None),
    )
    return jax.shard_map(
        on_device,
        mesh=mesh,
        in_specs=placed * 2,
        out_specs=(P("fsdp", "dp"),) * 6,
        check_vma=False,
    )
```

```python
import jax
import jax.numpy as jnp
from jax import lax
from jax.experimental import pallas as pl
from jax.experimental.pallas import tpu as pltpu
from jax.sharding import PartitionSpec as P

MESH = pl.DeviceIdType.MESH
BF16, F32 = jnp.bfloat16, jnp.float32

N_DP, NX, NLO, NZ = 4, 8, 2, 8
FF, TOK, D = 108, 256, 5120
COLS = D // N_DP
PAD = 112
ROWS = 2 * PAD
UNIT = 64
NEAREST = ((0, 2, 6, 4), (1, 7, 3, 5))
VMEM_LIMIT = 58 * 1024 * 1024


def fsdp_index(x, lo, z, core):
    return ((x * NLO + lo) * NZ + z) * 2 + core


def of_type_0(group):
    return (group == 0) | (group == 3)


def permutation(group):
    j = lax.broadcasted_iota(jnp.int32, (TOK, TOK), 0)
    place = lax.broadcasted_iota(jnp.int32, (TOK, TOK), 1)
    x_weight = jnp.where(of_type_0(group), 16, 64)
    moved = (j >> 6) * x_weight + ((j >> 2) & 3) * (80 - x_weight)
    moved = moved + ((j >> 5) & 1) * 8 + ((j >> 4) & 1) * 4 + (j & 3)
    return jnp.where(moved == place, 1.0, 0.0).astype(BF16)


def kernel(
    a_gate, a_up, a_cot, a_down, c_gate, c_up, c_cot, c_down,
    a_w, a_g, a_u, c_w, c_g, c_u,
    row_in, row_out, row_got, stage,
    gate_own, up_own, gate_sib, up_sib, down2, down, gate_f, up_f, hid, cot,
    hown, hsend, hgot, wout, gout, uout,
    load_sem, sib_send, sib_recv, p0_send, p0_recv, p1_send, p1_recv,
    ring_send, ring_recv, hid_send, hid_recv, rs_send, rs_recv, out_sem, out_send, out_recv,
):
    k = lax.axis_index("dp")
    f = lax.axis_index("fsdp")
    core = f % 2
    z = (f // 2) % NZ
    lo = (f // (2 * NZ)) % NLO
    x = f // (2 * NZ * NLO)
    xp, zp = x // 2, z // 2
    kind = (x + z) % 2
    held = x % 2 * 2 + z % 2
    sib = (k, f + 1 - 2 * core)

    def by_core(fn):
        @pl.when(core == 0)
        def _():
            fn(0)

        @pl.when(core == 1)
        def _():
            fn(1)

    gates, ups, downs = (a_gate, c_gate), (a_up, c_up), (a_down, c_down)
    cot_rows = (a_cot, c_cot)
    columns = pl.ds(pl.multiple_of(k * COLS, 128), COLS)

    row_loads = [pltpu.make_async_copy(cot_rows[m], row_in.at[m], load_sem.at[m]) for m in range(2)]
    for copy in row_loads:
        copy.start()

    def model_load(m, i):
        return pltpu.make_async_copy((gates[m], ups[m])[i], (gate_own, up_own)[i].at[m], load_sem.at[2 + 2 * i + m])

    def down_load(m):
        return pltpu.make_async_copy(downs[m].at[:, columns], down2.at[m], load_sem.at[6])

    for m in range(2):
        for i in range(2):
            model_load(m, i).start()
    by_core(lambda m: down_load(m).start())

    barrier = pltpu.get_barrier_semaphore()

    def greet(dp, fs):
        pl.semaphore_signal(barrier, inc=1, device_id=(dp, fs), device_id_type=MESH)

    own_p0 = held == k
    for a in range(16):
        source = fsdp_index(
            x // 2 * 2 + (x + a // 8 + 1) % 2, (lo + a // 4 + 1) % 2, z // 2 * 2 + (z + a // 2 + 1) % 2, (core + a + 1) % 2)
        if a < 15:
            greet(held, source)
        else:
            pl.when(jnp.logical_not(own_p0))(lambda source=source: greet(held, source))

    for i in range(4):
        @pl.when((kind == 1) | (i > 0))
        def _(i=i):
            greet(k, fsdp_index((x + 2 * i + kind) % NX, lo, z, core))

        @pl.when((kind == 0) | (i > 0))
        def _(i=i):
            greet(k, fsdp_index(x, lo, (z + 2 * i + 1 - kind) % NZ, core))

    for step in (1, NX - 1):
        greet(k, fsdp_index((x + step) % NX, lo, z, core))
        greet(k, fsdp_index(x, lo, (z + step) % NZ, core))
    for d in range(1, 4):
        greet((k + d) % N_DP, f)
        greet((k + d) % N_DP, sib[1])
    greet(*sib)

    for m in range(2):
        row_loads[m].wait()
        for b in range(N_DP):
            row_out[2 * b + m] = row_in[m, :, b * COLS:(b + 1) * COLS].astype(F32)

    pl.semaphore_wait(barrier, 34 - jnp.where(own_p0, 1, 0))

    mine = x % 2 * 8 + lo * 4 + z % 2 * 2 + core
    stage0 = []
    for away in (2, 1, 3, 0):
        for a in range(4):
            t_k, t_lo, t_core = (k + away) % N_DP, (lo + a // 2 + 1) % 2, (core + a + 1) % 2
            src = row_out.at[2 * t_k + t_core]
            stage0.append(pltpu.make_async_remote_copy(
                src, row_got.at[mine], p0_send.at[len(stage0)], p0_recv,
                device_id=(t_k, fsdp_index(2 * xp + k // 2, t_lo, 2 * zp + k % 2, t_core)), device_id_type=MESH))
            if len(stage0) < 16:
                stage0[-1].start()
            else:
                pl.when(own_p0)(lambda src=src: pltpu.make_async_copy(src, row_got.at[mine], p0_recv).start())
                pl.when(jnp.logical_not(own_p0))(stage0[-1].start)

    def sibling_push(m, i):
        src = (gates[1 - m], ups[1 - m], downs[1 - m].at[:, columns])[i]
        return pltpu.make_async_remote_copy(
            src, (gate_sib, up_sib, down2.at[m])[i], sib_send.at[i], sib_recv.at[i], device_id=sib, device_id_type=MESH)

    by_core(lambda m: [sibling_push(m, i).start() for i in range(3)])

    perm = permutation(k)

    for m in range(2):
        for i in range(2):
            model_load(m, i).wait()
    for m in range(2):
        gate32 = lax.dot_general(perm, gate_own[m], (((0,), (1,)), ((), ())), preferred_element_type=F32)
        up32 = lax.dot_general(perm, up_own[m], (((0,), (1,)), ((), ())), preferred_element_type=F32)
        sig = jax.nn.sigmoid(gate32)
        gate_f[m, :, :FF] = up32 * sig * (1.0 + gate32 * (1.0 - sig))
        up_f[m, :, :FF] = gate32 * sig

    pltpu.make_async_copy(row_got, row_got, p0_recv).wait()
    for r in range(16):
        stage[r:r + 1, :] = row_got[r]
    unit_at, block_at = jnp.where(kind == 0, zp, xp), jnp.where(kind == 0, xp, zp)
    cot[held, unit_at, block_at] = stage[...].astype(BF16)

    own_block = cot.at[held, unit_at, block_at]
    stage1 = []
    for d in (4, 5, 3, 6, 2, 7, 1):
        target = jnp.where(
            kind == 0, fsdp_index((x + d) % NX, lo, z, core), fsdp_index(x, lo, (z + d) % NZ, core))
        copy = pltpu.make_async_remote_copy(
            own_block, own_block, p1_send.at[d - 1], p1_recv.at[kind, block_at], device_id=(k, target), device_id_type=MESH)
        copy.start()
        stage1.append(copy)

    by_core(lambda m: [sibling_push(m, i).wait() for i in range(2)])
    for h, (gate, up) in enumerate(((gate_own[core], up_own[core]), (gate_sib[...], up_sib[...]))):
        gate32 = jnp.dot(gate, perm, preferred_element_type=F32)
        up32 = jnp.dot(up, perm, preferred_element_type=F32)
        hid[k, h * PAD:h * PAD + FF, :] = (gate32 * jax.nn.sigmoid(gate32) * up32).astype(BF16)

    hid_copies = []
    for d in range(1, 4):
        copy = pltpu.make_async_remote_copy(
            hid.at[k], hid.at[k], hid_send.at[d - 1], hid_recv.at[d - 1],
            device_id=((k + d) % N_DP, f), device_id_type=MESH)
        copy.start()
        hid_copies.append(copy)

    by_core(lambda m: [down_load(m).wait(), sibling_push(m, 2).wait()])
    for h in range(2):
        down[h * 128:h * 128 + FF, :] = down2[h]

    def unit_of(way, index):
        return (3 * (index % 2), index // 2) if way == 0 else (1 + index % 2, index // 2)

    def block_of(flow, i, step):
        shift = -step if flow % 2 == 0 else step
        along, across = (z, x) if flow < 2 else (x, z)
        index = (along + shift + 8) % 8
        has_own = (along + across + step) % 2 == flow // 2
        block = (across + jnp.where(has_own, NEAREST[0][i], NEAREST[1][i])) % 8 // 2
        group, unit = unit_of(flow // 2, index)
        return cot.at[group, unit, block], block

    def ring_copy(flow, i, step):
        forward = flow % 2 == 0
        ref, _ = block_of(flow, i, step)
        if flow < 2:
            target = fsdp_index(x, lo, (z + (1 if forward else NZ - 1)) % NZ, core)
        else:
            target = fsdp_index((x + (1 if forward else NX - 1)) % NX, lo, z, core)
        return pltpu.make_async_remote_copy(
            ref, ref, ring_send.at[flow, i, step], ring_recv.at[flow, i, step],
            device_id=(k, target), device_id_type=MESH)

    def block_wait(way, i):
        ref, at = block_of(2 * way, i, 0)

        def wait():
            pltpu.make_async_copy(ref, ref, p1_recv.at[way, at]).wait()

        if i:
            wait()
        else:
            pl.when(kind != way)(wait)

    def send_partial(way, index):
        index = (index + 8) % 8
        group, unit = unit_of(way, index)
        grad = lax.dot_general(
            cot[group, unit].reshape(UNIT, COLS), down[...], (((1,), (1,)), ((), ())), preferred_element_type=F32)
        apart = (group + N_DP - k) % N_DP
        for h in range(2):
            half = grad[:, h * 128:(h + 1) * 128].reshape(4, 16, 128)
            hsend[way, index, h] = half.astype(BF16)
            slot = jnp.where(core == h, apart - 1, apart + 3)

            @pl.when((apart != 0) | (core != h))
            def _(h=h, slot=slot):
                pltpu.make_async_remote_copy(
                    hsend.at[way, index, h], hgot.at[slot, unit], rs_send, rs_recv,
                    device_id=(group, f - core + h), device_id_type=MESH).start()

            @pl.when((apart == 0) & (core == h))
            def _(half=half):
                hown[unit] = half

    rings = {}
    for step, i in [(step, i) for step in range(5) for i in range(4)]:
        for flow in range(4):
            if step == 0 and flow % 2 == 0:
                block_wait(flow // 2, i)
            if (flow, i, step - 1) in rings:
                rings[flow, i, step - 1].wait_recv()
            if step < 3 or step == 3 and (i < 2) == (flow % 2 == 0):
                rings[flow, i, step] = ring_copy(flow, i, step)
                rings[flow, i, step].start()
        if i < 3:
            continue
        for shift in (-step, step) if 0 < step < 4 else (step,):
            send_partial(0, z + shift)
            send_partial(1, x + shift)

    for copy in hid_copies:
        copy.wait_recv()
    for n in range(COLS // 256):
        part = slice(n * 256, (n + 1) * 256)
        total = None
        for group in range(N_DP):
            term = jnp.dot(hid[group], cot[group, :, :, :, part].reshape(TOK, 256), preferred_element_type=F32)
            total = term if total is None else total + term
        wout[0, :, part] = total[:FF]
        wout[1, :, part] = total[PAD:PAD + FF]

    weights, ggrads, ugrads = (a_w, c_w), (a_g, c_g), (a_u, c_u)

    def weight_copies(m):
        return (
            pltpu.make_async_copy(wout.at[0], weights[m], out_sem.at[0]),
            pltpu.make_async_remote_copy(
                wout.at[1], weights[m], out_send, out_recv, device_id=sib, device_id_type=MESH),
        )

    by_core(lambda m: [copy.start() for copy in weight_copies(m)])

    pltpu.make_async_copy(hgot, hgot, rs_recv).wait()
    perm = permutation(k)
    for i, slots in enumerate(((0, 1, 2), (3, 4, 5, 6))):
        grad = hown[...] if i == 0 else 0.0
        for slot in slots:
            grad = grad + hgot[slot].astype(F32)
        grad = grad.reshape(TOK, 128)
        model = core if i == 0 else 1 - core
        for factor, out in ((gate_f, gout), (up_f, uout)):
            back = lax.dot_general(
                (grad * factor[model]).astype(BF16), perm, (((0,), (1,)), ((), ())), preferred_element_type=F32)
            out[i] = back[:FF].astype(BF16)

    def small_copies(m):
        return [
            pltpu.make_async_copy(src.at[i], outs[m if i == 0 else 1 - m], out_sem.at[1 + 2 * j + i])
            for i in range(2) for j, (src, outs) in enumerate(((gout, ggrads), (uout, ugrads)))
        ]

    by_core(lambda m: [copy.start() for copy in small_copies(m)])

    pl.when(jnp.logical_not(own_p0))(stage0.pop().wait_send)
    for copy in stage0 + stage1 + hid_copies + list(rings.values()):
        copy.wait_send()
    pltpu.make_async_copy(hgot, hgot, rs_send).wait()

    def finish(m):
        for copy in small_copies(m):
            copy.wait()
        local, remote = weight_copies(m)
        local.wait()
        remote.wait_send()
        pltpu.make_async_remote_copy(
            wout.at[1], weights[1 - m], out_send, out_recv, device_id=sib, device_id_type=MESH).wait_recv()

    by_core(finish)


def store(*refs):
    ins, outs, held, (in_sem, out_sem) = refs[:6], refs[6:12], refs[12:18], refs[18:]
    loads = [pltpu.make_async_copy(ins[i], held[i], in_sem.at[i]) for i in range(6)]
    stores = [pltpu.make_async_copy(held[i], outs[i], out_sem.at[i]) for i in range(6)]
    for copy in loads:
        copy.start()
    for load, copy in zip(loads, stores):
        load.wait()
        copy.start()
    for copy in stores:
        copy.wait()


def on_device(*args):
    hbm_spec = pl.BlockSpec(memory_space=pltpu.HBM)
    dma, vmem = pltpu.SemaphoreType.DMA, pltpu.VMEM
    weight = jax.ShapeDtypeStruct((FF, COLS), F32)
    small = jax.ShapeDtypeStruct((FF, TOK), BF16)
    results = pl.pallas_call(
        kernel,
        out_shape=(weight, small, small, weight, small, small),
        in_specs=[hbm_spec] * 8,
        out_specs=(hbm_spec,) * 6,
        scratch_shapes=[
            vmem((2, 1, D), BF16),
            vmem((8, 1, COLS), F32),
            vmem((16, 1, COLS), F32),
            vmem((16, COLS), F32),
            vmem((2, FF, TOK), BF16),
            vmem((2, FF, TOK), BF16),
            vmem((FF, TOK), BF16),
            vmem((FF, TOK), BF16),
            vmem((2, FF, COLS), BF16),
            vmem((256, COLS), BF16),
            vmem((2, TOK, 128), F32),
            vmem((2, TOK, 128), F32),
            vmem((N_DP, ROWS, TOK), BF16),
            vmem((N_DP, 4, 4, 16, COLS), BF16),
            vmem((4, 4, 16, 128), F32),
            vmem((2, 8, 2, 4, 16, 128), BF16),
            vmem((7, 4, 4, 16, 128), BF16),
            vmem((2, FF, COLS), F32),
            vmem((2, FF, TOK), BF16),
            vmem((2, FF, TOK), BF16),
            dma((7,)),
            dma((3,)),
            dma((3,)),
            dma((16,)),
            dma,
            dma((7,)),
            dma((2, 4)),
            dma((4, 4, 4)),
            dma((4, 4, 4)),
            dma((3,)),
            dma((3,)),
            dma,
            dma,
            dma((5,)),
            dma,
            dma,
        ],
        compiler_params=pltpu.CompilerParams(
            collective_id=0, has_side_effects=True, vmem_limit_bytes=VMEM_LIMIT),
        cost_estimate=pl.CostEstimate(flops=1_200_000_000, bytes_accessed=4_000_000, transcendentals=200_000),
        name="mlp_backward",
    )(*args)
    return pl.pallas_call(
        store,
        out_shape=(weight, small, small, weight, small, small),
        in_specs=[hbm_spec] * 6,
        out_specs=(hbm_spec,) * 6,
        scratch_shapes=[vmem(a.shape, a.dtype) for a in results] + [dma((6,)), dma((6,))],
        compiler_params=pltpu.CompilerParams(vmem_limit_bytes=VMEM_LIMIT),
        name="store_results",
    )(*results)


def solution(mesh):
    placed = (
        P("fsdp", "dp"),
        P("fsdp", "dp"),
        P(("dp", "fsdp"), None),
        P("fsdp", None),
    )
    return jax.shard_map(
        on_device,
        mesh=mesh,
        in_specs=placed * 2,
        out_specs=(P("fsdp", "dp"),) * 6,
        check_vma=False,
    )
```
